32 devices in a mesh: groups: 2 (over y), space: 8 (over z, core), tm: 2 (over x), rep: 1.
Axes of the slice: x: 2, y: 2, z: 4, core: 2. Of those that a mesh axis runs over, the one named last changes fastest.
Arguments:
- noise: float32 [8192, 4096], P(('groups', 'space'), 'tm'), parts along dimension 0, may hold values from -6 to 6
- factor: float32 [4096, 4096], P(('tm', 'rep'), 'space'), may hold values from -8 to 8, as said below
- col_blocks: int32 [64, 4], P(('groups', 'space')), parts along dimension 0, may hold values from 0 to 31, as said below
- block_values: float32 [64, 4, 128, 128], P(('groups', 'space')), parts along dimension 0, may hold values from -0.25 to 0.25
Outputs:
- samples: float32 [8192, 4096], P(('groups', 'space'), ('tm', 'rep')), parts along dimension 0
The draws below stay inside these ranges and needn't reach their ends.
There are 2 independent parts, one for each index of `groups`. The reference program is written for one: setup_inputs(seed, part) draws one part's arguments, and reference() takes and returns one part's arrays. A program takes and returns all parts, laid end to end along the dimension named above; an argument that names none is the same for every part. Nothing has to cross between parts.
Inputs may be any that keep to these rules, and one draw needn't show every extreme that they name: factor is lower triangular: every entry above the diagonal is zero, and the diagonal lies in 0.5 to 1.5. `col_blocks`: in every row b the first entry is b itself; the other 3 entries are distinct blocks whose circular distance from b (modulo 32) is 1 to 2.
All inputs are finite; a program needn't handle non-finite values.
Results may differ from the reference program's by a relative error of at most 0.0003.
Values sent between devices are 32-bit elements; how exact they have to be, the bound alone decides.
A program may use at most 128 MiB of HBM per device.

```python
import jax
import jax.numpy as jnp
from jax import lax

BS = 128
REACH = 2
HOURS = 4096
K = 4
NBLOCKS = 32
NODES = 4096


def draw_factor(key, part):
    first_key, second_key = jax.random.split(key, 2)
    rows = jnp.arange(HOURS)[:, None]
    cols = jnp.arange(HOURS)[None, :]
    entries = jnp.clip(jax.random.normal(first_key, (HOURS, HOURS), jnp.float32), -6.0, 6.0)
    scaled = entries / jnp.sqrt(rows.astype(jnp.float32) + 1.0)
    lower = jnp.where(cols < rows, scaled, 0.0)
    diagonal = jax.random.uniform(second_key, (HOURS,), jnp.float32, 0.5, 1.5)
    return (lower + jnp.diag(diagonal)).astype(jnp.float32)


def draw_col_blocks(key, part):
    base = jnp.arange(2 * REACH)
    offsets = base - REACH + (base >= REACH).astype(jnp.int32)
    scores = jax.random.randint(key, (NBLOCKS, 2 * REACH), 0, 1 << 20) * (2 * REACH) + base[None, :]
    order = jnp.argsort(scores, axis=1)[:, :K - 1]
    picked = offsets[order]
    own = jnp.arange(NBLOCKS)[:, None]
    others = (own + picked) % NBLOCKS
    return jnp.concatenate([own, others], axis=1).astype(jnp.int32)


def block_scale(key, shape, cuts, smallest, high):
    factor_of, own = 1.0, jax.random.fold_in(key, 6)
    for position, blocks in cuts:
        draws = jnp.exp(jax.random.uniform(jax.random.fold_in(own, position), (blocks,), jnp.float32, smallest / len(cuts), high / len(cuts)))
        factor_of = factor_of * jnp.repeat(draws, shape[position] // blocks).reshape([-1 if axis == position else 1 for axis in range(len(shape))])
    return factor_of


def centred(key, shape, scale, most, shards=(), dtype=jnp.bfloat16):
    array = jax.random.normal(key, shape, jnp.float32) * scale
    if len(shards) > 0:
        array = block_scale(key, shape, shards, -0.22, 0.18) * array
    return jnp.clip(array, min=-most, max=most).astype(dtype)


def setup_inputs(seed: int = 0, part: int = 0) -> dict:
    keys = jax.random.split(jax.random.key(seed), 5)
    part_splits = jax.random.split(jax.random.fold_in(keys[4], part), 5)
    noise = centred(part_splits[0], (NODES, HOURS), 1.0, 6.0, ((0, 8), (1, 2)), jnp.float32)
    factor = draw_factor(jax.random.fold_in(keys[4], 71), part)
    col_blocks = draw_col_blocks(jax.random.fold_in(jax.random.fold_in(keys[4], part), 71), part)
    block_values = centred(part_splits[3], (NBLOCKS, K, BS, BS), (K * BS) ** -0.5, 0.25, ((0, 8),), jnp.float32)
    return {"noise": noise, "factor": factor, "col_blocks": col_blocks, "block_values": block_values}


def reference(noise, factor, col_blocks, block_values):
    colored = jnp.dot(noise, factor.T, precision=lax.Precision.HIGHEST, preferred_element_type=jnp.float32)
    blocks = colored.reshape(NBLOCKS, BS, HOURS)

    def block_row(operands):
        columns, values = operands
        picked = blocks[columns.astype(jnp.int32)]
        return jnp.einsum("kab,kbh->ah", values.astype(jnp.float32), picked, precision=lax.Precision.HIGHEST)

    result = lax.map(block_row, (col_blocks, block_values))
    return result.reshape(NODES, HOURS)
```

```python
import functools

import jax
import jax.numpy as jnp
from jax import lax
from jax.experimental import pallas as pl
from jax.experimental.pallas import tpu as pltpu
from jax.sharding import PartitionSpec as P

BS = 128
REACH = 2


def shifted(block, axis, distance):
    devices = range(lax.axis_size(axis))
    route = [(i - distance, i) for i in devices if i - distance in devices]
    return lax.ppermute(block, axis, route)


def extended_2(block, sides, width):
    for axis, dim in sides:
        count = lax.axis_size(axis)
        forward = [(i, i + 1) for i in range(count - 1)]
        forward.append((count - 1, 0))
        backward = [(target, source) for source, target in forward]
        low = lax.ppermute(
            lax.slice_in_dim(block, block.shape[dim] - width, None, axis=dim), axis, forward
        )
        high = lax.ppermute(lax.slice_in_dim(block, 0, width, axis=dim), axis, backward)
        block = jnp.concatenate([low, block, high], axis=dim)
    return block


def per_device(noise, factor, col_blocks, block_values):
    node_rows = noise.shape[0]
    hour_cols = noise.shape[1]
    tm_index = lax.axis_index("tm")
    tm_count = lax.axis_size("tm")
    every_hour = jnp.zeros((node_rows, hour_cols * tm_count), jnp.float32)
    every_hour = lax.dynamic_update_slice_in_dim(every_hour, noise, tm_index * hour_cols, 1)
    moving = noise
    for step in range(1, tm_count):
        moving = shifted(moving, "tm", 1)
        slot = jnp.maximum(tm_index - step, 0) * hour_cols
        placed = lax.dynamic_update_slice_in_dim(every_hour, moving, slot, 1)
        every_hour = jnp.where(tm_index >= step, placed, every_hour)
    colored = lax.dot_general(
        every_hour,
        lax.all_gather(factor, "space", axis=1, tiled=True),
        (((1,), (1,)), ((), ())),
        precision=lax.Precision.HIGHEST,
        preferred_element_type=jnp.float32,
    )
    extended = extended_2(colored, (("space", 0),), REACH * BS)
    local_blocks = node_rows // BS
    out_cols = colored.shape[1]
    ext_blocks = extended.reshape(local_blocks + 2 * REACH, BS, out_cols)
    all_blocks = lax.axis_size("space") * local_blocks
    local_rows = jnp.arange(local_blocks, dtype=jnp.int32)[:, None]
    global_rows = lax.axis_index("space") * local_blocks + local_rows
    offsets = (col_blocks - global_rows + REACH) % all_blocks - REACH
    positions = local_rows + REACH + offsets
    picked = ext_blocks[positions]
    result = jnp.einsum("nkab,nkbh->nah", block_values, picked, precision=lax.Precision.HIGHEST)
    return result.reshape(node_rows, out_cols)


MESH = pl.DeviceIdType.MESH


def split(x):
    high = x.astype(jnp.bfloat16)
    return high, (x - high.astype(jnp.float32)).astype(jnp.bfloat16)


def dot3(a, b, dims):
    (ah, al), (bh, bl) = a, b
    dot = functools.partial(
        lax.dot_general, dimension_numbers=dims, preferred_element_type=jnp.float32
    )
    return dot(ah, bh) + (dot(ah, bl) + dot(al, bh))


def fused_kernel(
    count, noise, factor, cols, values, out,
    fac, ext, qn, wh, wl,
    s_chain, r_chain, s_other, r_other, s_halo, r_halo, s_qn, r_qn, s_loc, s_own,
):
    d, m, y = lax.axis_index("space"), lax.axis_index("tm"), lax.axis_index("groups")
    core = lax.rem(d, 2)
    width = factor.shape[1]
    half = width // 2
    hb = factor.shape[0] // width
    steps = count * hb
    rows = noise.shape[0]
    reach = REACH * BS
    local = rows // BS

    def at(**where):
        return {k: v for k, v in where.items()}

    right, left = lax.rem(d + 1, count), lax.rem(d + count - 1, count)
    sibling = d + 1 - 2 * core
    barrier = pltpu.get_barrier_semaphore()
    for where in (at(space=right), at(space=left), at(tm=1 - m), at(groups=1 - y)):
        pl.semaphore_signal(barrier, inc=1, device_id=where, device_id_type=MESH)

    def slot(i, j):
        a = i - hb
        return jnp.where(i < hb, i * hb + j, hb * hb + hb * a - a * (a - 1) // 2 + j - a)

    def valid(i, j):
        return (i >= 0) & (i < count) & (j >= i - hb * m)

    def rows_of(i, j, h):
        return fac.at[slot(i, j), pl.ds(pl.multiple_of(h * half, half), half), :]

    def chain(i, j, way):
        to = jnp.where(way == 0, right, left)
        return pltpu.make_async_remote_copy(
            src_ref=rows_of(i, j, y), dst_ref=rows_of(i, j, y),
            send_sem=s_chain.at[way, slot(i, j)], recv_sem=r_chain.at[slot(i, j)],
            device_id=at(space=to), device_id_type=MESH,
        )

    def cross(i, j):
        return pltpu.make_async_remote_copy(
            src_ref=rows_of(i, j, y), dst_ref=rows_of(i, j, y),
            send_sem=s_other.at[slot(i, j)], recv_sem=r_other.at[slot(i, j)],
            device_id=at(groups=1 - y), device_id_type=MESH,
        )

    def share(i, j):
        return pltpu.make_async_remote_copy(
            src_ref=rows_of(i, j, 1 - y), dst_ref=rows_of(i, j, 1 - y),
            send_sem=s_own.at[slot(i, j)], recv_sem=r_other.at[slot(i, j)],
            device_id=at(space=sibling), device_id_type=MESH,
        )

    def halo(c, way):
        if way == 0:
            src, dst, to = rows - reach, 0, right
        else:
            src, dst, to = 0, reach + rows, left
        return pltpu.make_async_remote_copy(
            src_ref=noise.at[pl.ds(src, reach), pl.ds(pl.multiple_of(c * width, width), width)],
            dst_ref=ext.at[c, pl.ds(dst, reach), :],
            send_sem=s_halo.at[way, c], recv_sem=r_halo.at[way, c],
            device_id=at(space=to), device_id_type=MESH,
        )

    def centre(c):
        return pltpu.make_async_copy(
            noise.at[:, pl.ds(c * width, width)], ext.at[c, pl.ds(reach, rows), :], s_loc.at[0, c]
        )

    def own_factor(j):
        return pltpu.make_async_copy(
            factor.at[pl.ds(j * width, width), :], fac.at[slot(d, j)], s_loc.at[1, j]
        )

    def give(c):
        return pltpu.make_async_remote_copy(
            src_ref=qn.at[c], dst_ref=qn.at[c], send_sem=s_qn.at[c], recv_sem=r_qn.at[c],
            device_id=at(tm=1 - m), device_id_type=MESH,
        )

    for j in range(hb):
        centre(j).start()
        pl.when(valid(d, j))(lambda j=j: own_factor(j).start())
    pl.semaphore_wait(barrier, 4)
    for c in reversed(range(hb)):
        halo(c, 0).start()
        halo(c, 1).start()

    for j in range(hb):
        @pl.when(valid(d, j))
        def _(j=j):
            own_factor(j).wait()
            pl.when(d < count - 1)(lambda: chain(d, j, 0).start())
            pl.when(d > 0)(lambda: chain(d, j, 1).start())
            share(d, j).start()

    out[...] = jnp.zeros_like(out)
    wh[...] = jnp.zeros_like(wh)
    wl[...] = jnp.zeros_like(wl)
    blocks = count * local
    for b in range(local):
        place = [
            lax.rem(cols[b, k] - (d * local + b) + REACH + blocks, blocks)
            for k in range(values.shape[1])
        ]
        for o in range(2 * REACH + 1):
            total = jnp.zeros((BS, BS), jnp.float32)
            for k, where in enumerate(place):
                total = total + values[b, k] * (where == o).astype(jnp.float32)
            high, low = split(total)
            wh[b * BS:(b + 1) * BS, (b + o) * BS:(b + o + 1) * BS] = high
            wl[b * BS:(b + 1) * BS, (b + o) * BS:(b + o + 1) * BS] = low
    for c in range(hb):
        centre(c).wait()

    def source(a, way):
        return jnp.where(way == 0, d - 1 - a, d + 1 + a)

    def apart(i):
        return i // 2 != d // 2

    def body(n, carry):
        a, j = n // hb, lax.rem(n, hb)
        for way in (0, 1):
            i = source(a, way)

            @pl.when(valid(i, j))
            def _(i=i, way=way):
                chain(i, j, way).wait_recv()
                more = (d < count - 1) if way == 0 else (d > 0)
                pl.when(more)(lambda: chain(i, j, way).start())
                pl.when(apart(i) & (lax.rem(j, 2) == core))(lambda: cross(i, j).start())

        before = jnp.maximum(n - 1, 0)
        b, k = before // hb, lax.rem(before, hb)
        for way in (0, 1):
            i = source(b, way)

            @pl.when((n > 0) & valid(i, k) & apart(i) & (lax.rem(k, 2) == core))
            def _(i=i):
                cross(i, k).wait_recv()
                share(i, k).start()

        @pl.when(n < hb)
        def _():
            c = hb - 1 - n
            halo(c, 0).wait_recv()
            halo(c, 1).wait_recv()
            q = dot3((wh[...], wl[...]), split(ext[c]), (((1,), (0,)), ((), ())))
            qn[m * hb + c] = q
            pl.when(m == 0)(lambda: give(c).start())

        for way in (0, 1):
            i = source(a - 1, way)

            @pl.when((a > 0) & valid(i, j) & ((lax.rem(j, 2) != core) | (i // 2 == d // 2)))
            def _(i=i):
                share(i, j).wait_recv()

        early = 2 * hb - a - 1 + 0 * j
        pl.when((j == 0) & (m == 1) & (a >= count - hb) & (a < count))(
            lambda: give(early).wait_recv()
        )

        def product(which, carry):
            i = jnp.where(
                which == 0, d - a, jnp.where(which == 1, d + a, jnp.where(which == 2, d, early))
            )
            late = (i >= hb) & (a > 0) & ((which != 2) | (a == 1))
            fits = jnp.where(which == 3, a >= count - hb, late)

            @pl.when(fits & valid(i, j))
            def _():
                at_cols = pl.ds(pl.multiple_of(j * width, width), width)
                out[:, at_cols] += dot3(
                    split(qn[i]), split(fac[slot(i, j)]), (((1,), (1,)), ((), ()))
                )

            return carry

        return lax.fori_loop(0, 4, product, carry)

    lax.fori_loop(0, steps, body, 0)

    for c in range(hb):
        halo(c, 0).wait_send()
        halo(c, 1).wait_send()
        pl.when(m == 0)(lambda c=c: give(c).wait_send())

    def drain(n, carry):
        i, j = n // hb, lax.rem(n, hb)

        @pl.when(valid(i, j))
        def _():
            pl.when((i <= d) & (d < count - 1))(lambda: chain(i, j, 0).wait_send())
            pl.when((i >= d) & (d > 0))(lambda: chain(i, j, 1).wait_send())
            mine = apart(i) & (lax.rem(j, 2) == core)
            pl.when(mine)(lambda: cross(i, j).wait_send())
            pl.when(mine | (i == d))(lambda: share(i, j).wait_send())

        return carry

    lax.fori_loop(0, steps, drain, 0)


def fused(noise, factor, col_blocks, block_values):
    count = lax.axis_size("space")
    rows, width = noise.shape[0], factor.shape[1]
    hb = factor.shape[0] // width
    slots = hb * hb + hb * (hb + 1) // 2
    dma = pltpu.SemaphoreType.DMA
    return pl.pallas_call(
        functools.partial(fused_kernel, count),
        out_shape=jax.ShapeDtypeStruct(noise.shape, jnp.float32),
        in_specs=[
            pl.BlockSpec(memory_space=pl.ANY),
            pl.BlockSpec(memory_space=pl.ANY),
            pl.BlockSpec(memory_space=pltpu.SMEM),
            pl.BlockSpec(memory_space=pltpu.VMEM),
        ],
        out_specs=pl.BlockSpec(memory_space=pltpu.VMEM),
        scratch_shapes=[
            pltpu.VMEM((slots, width, width), jnp.float32),
            pltpu.VMEM((hb, rows + 2 * REACH * BS, width), jnp.float32),
            pltpu.VMEM((2 * hb, rows, width), jnp.float32),
            pltpu.VMEM((rows, rows + 2 * REACH * BS), jnp.bfloat16),
            pltpu.VMEM((rows, rows + 2 * REACH * BS), jnp.bfloat16),
            dma((2, slots)), dma((slots,)), dma((slots,)), dma((slots,)),
            dma((2, hb)), dma((2, hb)), dma((2 * hb,)), dma((2 * hb,)),
            dma((2, hb)), dma((slots,)),
        ],
        compiler_params=pltpu.CompilerParams(
            collective_id=0, has_side_effects=True, vmem_limit_bytes=62 * 1024 * 1024
        ),
    )(noise, factor, col_blocks, block_values)


def fits_fused(mesh):
    shape = mesh.shape
    return (
        shape["tm"] == 2 and shape["rep"] == 1 and shape["groups"] == 2
        and shape["space"] % 2 == 0 and shape["space"] >= 4
    )


def solution(mesh):
    return jax.shard_map(
        fused if fits_fused(mesh) else per_device,
        mesh=mesh,
        in_specs=(
            P(("groups", "space"), "tm"),
            P(("tm", "rep"), "space"),
            P(("groups", "space"), None),
            P(("groups", "space"), None, None, None),
        ),
        out_specs=P(("groups", "space"), ("tm", "rep")),
        check_vma=False,
    )
```

```python
import functools

import jax
import jax.numpy as jnp
from jax import lax
from jax.experimental import pallas as pl
from jax.experimental.pallas import tpu as pltpu
from jax.sharding import PartitionSpec as P

BS = 128
REACH = 2


def shifted(block, axis, distance):
    devices = range(lax.axis_size(axis))
    route = [(i - distance, i) for i in devices if i - distance in devices]
    return lax.ppermute(block, axis, route)


def extended_2(block, sides, width):
    for axis, dim in sides:
        count = lax.axis_size(axis)
        forward = [(i, i + 1) for i in range(count - 1)]
        forward.append((count - 1, 0))
        backward = [(target, source) for source, target in forward]
        low = lax.ppermute(
            lax.slice_in_dim(block, block.shape[dim] - width, None, axis=dim), axis, forward
        )
        high = lax.ppermute(lax.slice_in_dim(block, 0, width, axis=dim), axis, backward)
        block = jnp.concatenate([low, block, high], axis=dim)
    return block


def per_device(noise, factor, col_blocks, block_values):
    node_rows = noise.shape[0]
    hour_cols = noise.shape[1]
    tm_index = lax.axis_index("tm")
    tm_count = lax.axis_size("tm")
    every_hour = jnp.zeros((node_rows, hour_cols * tm_count), jnp.float32)
    every_hour = lax.dynamic_update_slice_in_dim(every_hour, noise, tm_index * hour_cols, 1)
    moving = noise
    for step in range(1, tm_count):
        moving = shifted(moving, "tm", 1)
        slot = jnp.maximum(tm_index - step, 0) * hour_cols
        placed = lax.dynamic_update_slice_in_dim(every_hour, moving, slot, 1)
        every_hour = jnp.where(tm_index >= step, placed, every_hour)
    colored = lax.dot_general(
        every_hour,
        lax.all_gather(factor, "space", axis=1, tiled=True),
        (((1,), (1,)), ((), ())),
        precision=lax.Precision.HIGHEST,
        preferred_element_type=jnp.float32,
    )
    extended = extended_2(colored, (("space", 0),), REACH * BS)
    local_blocks = node_rows // BS
    out_cols = colored.shape[1]
    ext_blocks = extended.reshape(local_blocks + 2 * REACH, BS, out_cols)
    all_blocks = lax.axis_size("space") * local_blocks
    local_rows = jnp.arange(local_blocks, dtype=jnp.int32)[:, None]
    global_rows = lax.axis_index("space") * local_blocks + local_rows
    offsets = (col_blocks - global_rows + REACH) % all_blocks - REACH
    positions = local_rows + REACH + offsets
    picked = ext_blocks[positions]
    result = jnp.einsum("nkab,nkbh->nah", block_values, picked, precision=lax.Precision.HIGHEST)
    return result.reshape(node_rows, out_cols)


MESH = pl.DeviceIdType.MESH


def split(x):
    high = x.astype(jnp.bfloat16)
    return high, (x - high.astype(jnp.float32)).astype(jnp.bfloat16)


def dot3(a, b, dims):
    (ah, al), (bh, bl) = a, b
    dot = functools.partial(
        lax.dot_general, dimension_numbers=dims, preferred_element_type=jnp.float32
    )
    return dot(ah, bh) + (dot(ah, bl) + dot(al, bh))


def fused_kernel(
    count, noise, factor, cols, values, out,
    fac, ext, qn, wh, wl,
    s_chain, r_chain, s_other, r_other, s_halo, r_halo, s_qn, r_qn, s_loc, s_own,
):
    d, m, y = lax.axis_index("space"), lax.axis_index("tm"), lax.axis_index("groups")
    core = lax.rem(d, 2)
    width = factor.shape[1]
    half = width // 2
    hb = factor.shape[0] // width
    steps = count * hb
    rows = noise.shape[0]
    reach = REACH * BS
    local = rows // BS

    def at(**where):
        return {k: v for k, v in where.items()}

    right, left = lax.rem(d + 1, count), lax.rem(d + count - 1, count)
    sibling = d + 1 - 2 * core
    barrier = pltpu.get_barrier_semaphore()
    for where in (at(space=right), at(space=left), at(tm=1 - m), at(groups=1 - y)):
        pl.semaphore_signal(barrier, inc=1, device_id=where, device_id_type=MESH)

    def slot(i, j):
        a = i - hb
        return jnp.where(i < hb, i * hb + j, hb * hb + hb * a - a * (a - 1) // 2 + j - a)

    def valid(i, j):
        return (i >= 0) & (i < count) & (j >= i - hb * m)

    def rows_of(i, j, h):
        return fac.at[slot(i, j), pl.ds(pl.multiple_of(h * half, half), half), :]

    def chain(i, j, way):
        to = jnp.where(way == 0, right, left)
        return pltpu.make_async_remote_copy(
            src_ref=rows_of(i, j, y), dst_ref=rows_of(i, j, y),
            send_sem=s_chain.at[way, slot(i, j)], recv_sem=r_chain.at[slot(i, j)],
            device_id=at(space=to), device_id_type=MESH,
        )

    def cross(i, j):
        return pltpu.make_async_remote_copy(
            src_ref=rows_of(i, j, y), dst_ref=rows_of(i, j, y),
            send_sem=s_other.at[slot(i, j)], recv_sem=r_other.at[slot(i, j)],
            device_id=at(groups=1 - y), device_id_type=MESH,
        )

    def share(i, j):
        return pltpu.make_async_remote_copy(
            src_ref=rows_of(i, j, 1 - y), dst_ref=rows_of(i, j, 1 - y),
            send_sem=s_own.at[slot(i, j)], recv_sem=r_other.at[slot(i, j)],
            device_id=at(space=sibling), device_id_type=MESH,
        )

    def halo(c, way):
        if way == 0:
            src, dst, to = rows - reach, 0, right
        else:
            src, dst, to = 0, reach + rows, left
        return pltpu.make_async_remote_copy(
            src_ref=noise.at[pl.ds(src, reach), pl.ds(pl.multiple_of(c * width, width), width)],
            dst_ref=ext.at[c, pl.ds(dst, reach), :],
            send_sem=s_halo.at[way, c], recv_sem=r_halo.at[way, c],
            device_id=at(space=to), device_id_type=MESH,
        )

    def centre(c):
        return pltpu.make_async_copy(
            noise.at[:, pl.ds(c * width, width)], ext.at[c, pl.ds(reach, rows), :], s_loc.at[0, c]
        )

    def own_factor(j):
        return pltpu.make_async_copy(
            factor.at[pl.ds(j * width, width), :], fac.at[slot(d, j)], s_loc.at[1, j]
        )

    def give(c):
        return pltpu.make_async_remote_copy(
            src_ref=qn.at[c], dst_ref=qn.at[c], send_sem=s_qn.at[c], recv_sem=r_qn.at[c],
            device_id=at(tm=1 - m), device_id_type=MESH,
        )

    for j in range(hb):
        centre(j).start()
        pl.when(valid(d, j))(lambda j=j: own_factor(j).start())
    pl.semaphore_wait(barrier, 4)
    for j in range(hb):
        halo(hb - 1 - j, 0).start()
        halo(hb - 1 - j, 1).start()

        @pl.when(valid(d, j))
        def _(j=j):
            own_factor(j).wait()
            pl.when(d < count - 1)(lambda: chain(d, j, 0).start())
            pl.when(d > 0)(lambda: chain(d, j, 1).start())
            share(d, j).start()

    out[...] = jnp.zeros_like(out)
    wh[...] = jnp.zeros_like(wh)
    wl[...] = jnp.zeros_like(wl)
    blocks = count * local
    for b in range(local):
        place = [
            lax.rem(cols[b, k] - (d * local + b) + REACH + blocks, blocks)
            for k in range(values.shape[1])
        ]
        for o in range(2 * REACH + 1):
            total = jnp.zeros((BS, BS), jnp.float32)
            for k, where in enumerate(place):
                total = total + values[b, k] * (where == o).astype(jnp.float32)
            high, low = split(total)
            wh[b * BS:(b + 1) * BS, (b + o) * BS:(b + o + 1) * BS] = high
            wl[b * BS:(b + 1) * BS, (b + o) * BS:(b + o + 1) * BS] = low
    for c in range(hb):
        centre(c).wait()

    def source(a, way):
        return jnp.where(way == 0, d - 1 - a, d + 1 + a)

    def apart(i):
        return i // 2 != d // 2

    def body(n, carry):
        a, j = n // hb, lax.rem(n, hb)
        for way in (0, 1):
            i = source(a, way)

            @pl.when(valid(i, j))
            def _(i=i, way=way):
                chain(i, j, way).wait_recv()
                more = (d < count - 1) if way == 0 else (d > 0)
                pl.when(more)(lambda: chain(i, j, way).start())
                pl.when(apart(i) & (lax.rem(j, 2) == core))(lambda: cross(i, j).start())

        before = jnp.maximum(n - 1, 0)
        b, k = before // hb, lax.rem(before, hb)
        for way in (0, 1):
            i = source(b, way)

            @pl.when((n > 0) & valid(i, k) & apart(i) & (lax.rem(k, 2) == core))
            def _(i=i):
                cross(i, k).wait_recv()
                share(i, k).start()

        @pl.when((lax.rem(n, hb - 1) == 0) & (n > 0) & (n <= hb * (hb - 1)))
        def _():
            c = hb - n // (hb - 1)
            halo(c, 0).wait_recv()
            halo(c, 1).wait_recv()
            q = dot3((wh[...], wl[...]), split(ext[c]), (((1,), (0,)), ((), ())))
            qn[m * hb + c] = q
            pl.when(m == 0)(lambda: give(c).start())

        for way in (0, 1):
            i = source(a - 1, way)

            @pl.when((a > 0) & valid(i, j) & ((lax.rem(j, 2) != core) | (i // 2 == d // 2)))
            def _(i=i):
                share(i, j).wait_recv()

        early = 2 * hb - a - 1 + 0 * j
        pl.when((j == 0) & (m == 1) & (a >= count - hb) & (a < count))(
            lambda: give(early).wait_recv()
        )

        def product(which, carry):
            i = jnp.where(which == hb, early, hb + which)
            away = jnp.maximum(jnp.maximum(d - i, i - d), count - hb)
            fits = jnp.where(which == hb, a >= count - hb, a == away)

            @pl.when(fits & valid(i, j))
            def _():
                at_cols = pl.ds(pl.multiple_of(j * width, width), width)
                out[:, at_cols] += dot3(
                    split(qn[i]), split(fac[slot(i, j)]), (((1,), (1,)), ((), ()))
                )

            return carry

        return lax.fori_loop(0, hb + 1, product, carry)

    lax.fori_loop(0, steps, body, 0)

    for c in range(hb):
        halo(c, 0).wait_send()
        halo(c, 1).wait_send()
        pl.when(m == 0)(lambda c=c: give(c).wait_send())

    def drain(n, carry):
        i, j = n // hb, lax.rem(n, hb)

        @pl.when(valid(i, j))
        def _():
            pl.when((i <= d) & (d < count - 1))(lambda: chain(i, j, 0).wait_send())
            pl.when((i >= d) & (d > 0))(lambda: chain(i, j, 1).wait_send())
            mine = apart(i) & (lax.rem(j, 2) == core)
            pl.when(mine)(lambda: cross(i, j).wait_send())
            pl.when(mine | (i == d))(lambda: share(i, j).wait_send())

        return carry

    lax.fori_loop(0, steps, drain, 0)


def fused(noise, factor, col_blocks, block_values):
    count = lax.axis_size("space")
    rows, width = noise.shape[0], factor.shape[1]
    hb = factor.shape[0] // width
    slots = hb * hb + hb * (hb + 1) // 2
    dma = pltpu.SemaphoreType.DMA
    return pl.pallas_call(
        functools.partial(fused_kernel, count),
        out_shape=jax.ShapeDtypeStruct(noise.shape, jnp.float32),
        in_specs=[
            pl.BlockSpec(memory_space=pl.ANY),
            pl.BlockSpec(memory_space=pl.ANY),
            pl.BlockSpec(memory_space=pltpu.SMEM),
            pl.BlockSpec(memory_space=pltpu.VMEM),
        ],
        out_specs=pl.BlockSpec(memory_space=pltpu.VMEM),
        scratch_shapes=[
            pltpu.VMEM((slots, width, width), jnp.float32),
            pltpu.VMEM((hb, rows + 2 * REACH * BS, width), jnp.float32),
            pltpu.VMEM((2 * hb, rows, width), jnp.float32),
            pltpu.VMEM((rows, rows + 2 * REACH * BS), jnp.bfloat16),
            pltpu.VMEM((rows, rows + 2 * REACH * BS), jnp.bfloat16),
            dma((2, slots)), dma((slots,)), dma((slots,)), dma((slots,)),
            dma((2, hb)), dma((2, hb)), dma((2 * hb,)), dma((2 * hb,)),
            dma((2, hb)), dma((slots,)),
        ],
        compiler_params=pltpu.CompilerParams(
            collective_id=0, has_side_effects=True, vmem_limit_bytes=62 * 1024 * 1024
        ),
    )(noise, factor, col_blocks, block_values)


def fits_fused(mesh):
    shape = mesh.shape
    return (
        shape["tm"] == 2 and shape["rep"] == 1 and shape["groups"] == 2
        and shape["space"] % 2 == 0 and shape["space"] >= 4
    )


def solution(mesh):
    return jax.shard_map(
        fused if fits_fused(mesh) else per_device,
        mesh=mesh,
        in_specs=(
            P(("groups", "space"), "tm"),
            P(("tm", "rep"), "space"),
            P(("groups", "space"), None),
            P(("groups", "space"), None, None, None),
        ),
        out_specs=P(("groups", "space"), ("tm", "rep")),
        check_vma=False,
    )
```

```python
import functools

import jax
import jax.numpy as jnp
from jax import lax
from jax.experimental import pallas as pl
from jax.experimental.pallas import tpu as pltpu
from jax.sharding import PartitionSpec as P

BS = 128
REACH = 2


def shifted(block, axis, distance):
    devices = range(lax.axis_size(axis))
    route = [(i - distance, i) for i in devices if i - distance in devices]
    return lax.ppermute(block, axis, route)


def extended_2(block, sides, width):
    for axis, dim in sides:
        count = lax.axis_size(axis)
        forward = [(i, i + 1) for i in range(count - 1)]
        forward.append((count - 1, 0))
        backward = [(target, source) for source, target in forward]
        low = lax.ppermute(
            lax.slice_in_dim(block, block.shape[dim] - width, None, axis=dim), axis, forward
        )
        high = lax.ppermute(lax.slice_in_dim(block, 0, width, axis=dim), axis, backward)
        block = jnp.concatenate([low, block, high], axis=dim)
    return block


def per_device(noise, factor, col_blocks, block_values):
    node_rows = noise.shape[0]
    hour_cols = noise.shape[1]
    tm_index = lax.axis_index("tm")
    tm_count = lax.axis_size("tm")
    every_hour = jnp.zeros((node_rows, hour_cols * tm_count), jnp.float32)
    every_hour = lax.dynamic_update_slice_in_dim(every_hour, noise, tm_index * hour_cols, 1)
    moving = noise
    for step in range(1, tm_count):
        moving = shifted(moving, "tm", 1)
        slot = jnp.maximum(tm_index - step, 0) * hour_cols
        placed = lax.dynamic_update_slice_in_dim(every_hour, moving, slot, 1)
        every_hour = jnp.where(tm_index >= step, placed, every_hour)
    colored = lax.dot_general(
        every_hour,
        lax.all_gather(factor, "space", axis=1, tiled=True),
        (((1,), (1,)), ((), ())),
        precision=lax.Precision.HIGHEST,
        preferred_element_type=jnp.float32,
    )
    extended = extended_2(colored, (("space", 0),), REACH * BS)
    local_blocks = node_rows // BS
    out_cols = colored.shape[1]
    ext_blocks = extended.reshape(local_blocks + 2 * REACH, BS, out_cols)
    all_blocks = lax.axis_size("space") * local_blocks
    local_rows = jnp.arange(local_blocks, dtype=jnp.int32)[:, None]
    global_rows = lax.axis_index("space") * local_blocks + local_rows
    offsets = (col_blocks - global_rows + REACH) % all_blocks - REACH
    positions = local_rows + REACH + offsets
    picked = ext_blocks[positions]
    result = jnp.einsum("nkab,nkbh->nah", block_values, picked, precision=lax.Precision.HIGHEST)
    return result.reshape(node_rows, out_cols)


MESH = pl.DeviceIdType.MESH


def split(x):
    high = x.astype(jnp.bfloat16)
    return high, (x - high.astype(jnp.float32)).astype(jnp.bfloat16)


def dot3(a, b, dims):
    (ah, al), (bh, bl) = a, b
    dot = functools.partial(
        lax.dot_general, dimension_numbers=dims, preferred_element_type=jnp.float32
    )
    return dot(ah, bh) + (dot(ah, bl) + dot(al, bh))


def fused_kernel(
    count, noise, factor, cols, values, out,
    fac, ext, qn, wh, wl,
    s_chain, r_chain, s_other, r_other, s_halo, r_halo, s_qn, r_qn, s_loc, s_own,
):
    d, m, y = lax.axis_index("space"), lax.axis_index("tm"), lax.axis_index("groups")
    core = lax.rem(d, 2)
    width = factor.shape[1]
    half = width // 2
    hb = factor.shape[0] // width
    steps = count * hb
    rows = noise.shape[0]
    reach = REACH * BS
    local = rows // BS

    def at(**where):
        return {k: v for k, v in where.items()}

    right, left = lax.rem(d + 1, count), lax.rem(d + count - 1, count)
    sibling = d + 1 - 2 * core
    barrier = pltpu.get_barrier_semaphore()
    for where in (at(space=right), at(space=left), at(tm=1 - m), at(groups=1 - y)):
        pl.semaphore_signal(barrier, inc=1, device_id=where, device_id_type=MESH)

    def slot(i, j):
        a = i - hb
        return jnp.where(i < hb, i * hb + j, hb * hb + hb * a - a * (a - 1) // 2 + j - a)

    def valid(i, j):
        return (i >= 0) & (i < count) & (j >= i - hb * m)

    def rows_of(i, j, h):
        return fac.at[slot(i, j), pl.ds(pl.multiple_of(h * half, half), half), :]

    def chain(i, j, way):
        to = jnp.where(way == 0, right, left)
        return pltpu.make_async_remote_copy(
            src_ref=rows_of(i, j, y), dst_ref=rows_of(i, j, y),
            send_sem=s_chain.at[way, slot(i, j)], recv_sem=r_chain.at[slot(i, j)],
            device_id=at(space=to), device_id_type=MESH,
        )

    def cross(i, j):
        return pltpu.make_async_remote_copy(
            src_ref=rows_of(i, j, y), dst_ref=rows_of(i, j, y),
            send_sem=s_other.at[slot(i, j)], recv_sem=r_other.at[slot(i, j)],
            device_id=at(groups=1 - y), device_id_type=MESH,
        )

    def share(i, j):
        return pltpu.make_async_remote_copy(
            src_ref=rows_of(i, j, 1 - y), dst_ref=rows_of(i, j, 1 - y),
            send_sem=s_own.at[slot(i, j)], recv_sem=r_other.at[slot(i, j)],
            device_id=at(space=sibling), device_id_type=MESH,
        )

    def halo(c, way):
        if way == 0:
            src, dst, to = rows - reach, 0, right
        else:
            src, dst, to = 0, reach + rows, left
        return pltpu.make_async_remote_copy(
            src_ref=noise.at[pl.ds(src, reach), pl.ds(pl.multiple_of(c * width, width), width)],
            dst_ref=ext.at[c, pl.ds(dst, reach), :],
            send_sem=s_halo.at[way, c], recv_sem=r_halo.at[way, c],
            device_id=at(space=to), device_id_type=MESH,
        )

    def centre(c):
        return pltpu.make_async_copy(
            noise.at[:, pl.ds(c * width, width)], ext.at[c, pl.ds(reach, rows), :], s_loc.at[0, c]
        )

    def own_factor(j):
        return pltpu.make_async_copy(
            factor.at[pl.ds(j * width, width), :], fac.at[slot(d, j)], s_loc.at[1, j]
        )

    def give(c):
        return pltpu.make_async_remote_copy(
            src_ref=qn.at[c], dst_ref=qn.at[c], send_sem=s_qn.at[c], recv_sem=r_qn.at[c],
            device_id=at(tm=1 - m), device_id_type=MESH,
        )

    for j in range(hb):
        centre(j).start()
        pl.when(valid(d, j))(lambda j=j: own_factor(j).start())
    pl.semaphore_wait(barrier, 4)
    for j in range(hb):
        halo(hb - 1 - j, 0).start()
        halo(hb - 1 - j, 1).start()

        @pl.when(valid(d, j))
        def _(j=j):
            own_factor(j).wait()
            pl.when(d < count - 1)(lambda: chain(d, j, 0).start())
            pl.when(d > 0)(lambda: chain(d, j, 1).start())
            share(d, j).start()

    out[...] = jnp.zeros_like(out)
    wh[...] = jnp.zeros_like(wh)
    wl[...] = jnp.zeros_like(wl)
    blocks = count * local
    for b in range(local):
        place = [
            lax.rem(cols[b, k] - (d * local + b) + REACH + blocks, blocks)
            for k in range(values.shape[1])
        ]
        for o in range(2 * REACH + 1):
            total = jnp.zeros((BS, BS), jnp.float32)
            for k, where in enumerate(place):
                total = total + values[b, k] * (where == o).astype(jnp.float32)
            high, low = split(total)
            wh[b * BS:(b + 1) * BS, (b + o) * BS:(b + o + 1) * BS] = high
            wl[b * BS:(b + 1) * BS, (b + o) * BS:(b + o + 1) * BS] = low
    for c in range(hb):
        centre(c).wait()

    def source(a, way):
        return jnp.where(way == 0, d - 1 - a, d + 1 + a)

    def apart(i):
        return i // 2 != d // 2

    def body(n, carry):
        a, j = n // hb, lax.rem(n, hb)
        for way in (0, 1):
            i = source(a, way)

            @pl.when(valid(i, j))
            def _(i=i, way=way):
                chain(i, j, way).wait_recv()
                more = (d < count - 1) if way == 0 else (d > 0)
                pl.when(more)(lambda: chain(i, j, way).start())
                pl.when(apart(i) & (lax.rem(j, 2) == core))(lambda: cross(i, j).start())

        before = jnp.maximum(n - 3, 0)
        b, k = before // hb, lax.rem(before, hb)
        for way in (0, 1):
            i = source(b, way)

            @pl.when((n >= 3) & valid(i, k) & apart(i) & (lax.rem(k, 2) == core))
            def _(i=i):
                cross(i, k).wait_recv()
                share(i, k).start()

        @pl.when((lax.rem(n, hb - 1) == 0) & (n > 0) & (n <= hb * (hb - 1)))
        def _():
            c = hb - n // (hb - 1)
            halo(c, 0).wait_recv()
            halo(c, 1).wait_recv()
            q = dot3((wh[...], wl[...]), split(ext[c]), (((1,), (0,)), ((), ())))
            qn[m * hb + c] = q
            pl.when(m == 0)(lambda: give(c).start())

        for way in (0, 1):
            i = source(a - 2, way)

            @pl.when((a > 1) & valid(i, j) & ((lax.rem(j, 2) != core) | (i // 2 == d // 2)))
            def _(i=i):
                share(i, j).wait_recv()

        early = 2 * hb - a
        pl.when((j == 0) & (m == 1) & (a > count - hb) & (a <= count))(
            lambda: give(early).wait_recv()
        )

        def product(which, carry):
            i = jnp.where(which == hb, early, hb + which)
            away = jnp.maximum(jnp.maximum(d - i, i - d), count - hb)
            fits = jnp.where(which == hb, a > count - hb, a == away + 1)

            @pl.when(fits & valid(i, j))
            def _():
                at_cols = pl.ds(pl.multiple_of(j * width, width), width)
                out[:, at_cols] += dot3(
                    split(qn[i]), split(fac[slot(i, j)]), (((1,), (1,)), ((), ()))
                )

            return carry

        return lax.fori_loop(0, hb + 1, product, carry)

    lax.fori_loop(0, steps + hb, body, 0)

    for c in range(hb):
        halo(c, 0).wait_send()
        halo(c, 1).wait_send()
        pl.when(m == 0)(lambda c=c: give(c).wait_send())

    def drain(n, carry):
        i, j = n // hb, lax.rem(n, hb)

        @pl.when(valid(i, j))
        def _():
            pl.when((i <= d) & (d < count - 1))(lambda: chain(i, j, 0).wait_send())
            pl.when((i >= d) & (d > 0))(lambda: chain(i, j, 1).wait_send())
            mine = apart(i) & (lax.rem(j, 2) == core)
            pl.when(mine)(lambda: cross(i, j).wait_send())
            pl.when(mine | (i == d))(lambda: share(i, j).wait_send())

        return carry

    lax.fori_loop(0, steps, drain, 0)


def fused(noise, factor, col_blocks, block_values):
    count = lax.axis_size("space")
    rows, width = noise.shape[0], factor.shape[1]
    hb = factor.shape[0] // width
    slots = hb * hb + hb * (hb + 1) // 2
    dma = pltpu.SemaphoreType.DMA
    return pl.pallas_call(
        functools.partial(fused_kernel, count),
        out_shape=jax.ShapeDtypeStruct(noise.shape, jnp.float32),
        in_specs=[
            pl.BlockSpec(memory_space=pl.ANY),
            pl.BlockSpec(memory_space=pl.ANY),
            pl.BlockSpec(memory_space=pltpu.SMEM),
            pl.BlockSpec(memory_space=pltpu.VMEM),
        ],
        out_specs=pl.BlockSpec(memory_space=pltpu.VMEM),
        scratch_shapes=[
            pltpu.VMEM((slots, width, width), jnp.float32),
            pltpu.VMEM((hb, rows + 2 * REACH * BS, width), jnp.float32),
            pltpu.VMEM((2 * hb, rows, width), jnp.float32),
            pltpu.VMEM((rows, rows + 2 * REACH * BS), jnp.bfloat16),
            pltpu.VMEM((rows, rows + 2 * REACH * BS), jnp.bfloat16),
            dma((2, slots)), dma((slots,)), dma((slots,)), dma((slots,)),
            dma((2, hb)), dma((2, hb)), dma((2 * hb,)), dma((2 * hb,)),
            dma((2, hb)), dma((slots,)),
        ],
        compiler_params=pltpu.CompilerParams(
            collective_id=0, has_side_effects=True, vmem_limit_bytes=62 * 1024 * 1024
        ),
    )(noise, factor, col_blocks, block_values)


def fits_fused(mesh):
    shape = mesh.shape
    return (
        shape["tm"] == 2 and shape["rep"] == 1 and shape["groups"] == 2
        and shape["space"] % 2 == 0 and shape["space"] >= 4
    )


def solution(mesh):
    return jax.shard_map(
        fused if fits_fused(mesh) else per_device,
        mesh=mesh,
        in_specs=(
            P(("groups", "space"), "tm"),
            P(("tm", "rep"), "space"),
            P(("groups", "space"), None),
            P(("groups", "space"), None, None, None),
        ),
        out_specs=P(("groups", "space"), ("tm", "rep")),
        check_vma=False,
    )
```
